1024 devices in a mesh: rep: 64 (over x_hi, z, core), fsdp: 16 (over y, x_lo).
Axes of the slice: x: 8 (x_hi: 4, x_lo: 2; x = x_hi * 2 + x_lo), y: 8, z: 8, core: 2. Of those that a mesh axis runs over, the one named last changes fastest.
Arguments:
- tokens: bfloat16 [131072, 3072], P(('rep', 'fsdp')), may hold values from -6 to 6
- cotangent: bfloat16 [131072, 1024], P(('rep', 'fsdp')), may hold values from -0.13258252 to 0.13258252
- norm_gain: float32 [3072], replicated, may hold values from 0.5 to 9.2, as said below
- replica_drift: float32 [64, 3072, 1024], P('rep', 'fsdp'), may hold values from -3 to 3
- exponents: int32 [64, 3072, 8], P('rep', 'fsdp'), may hold values from 1 to 3
- global_weight: float32 [3072, 1024], P('fsdp'), may hold values from -6 to 6
- momentum: float32 [16, 64, 3, 1024], P('fsdp', 'rep'), may hold values from -3 to 3
Outputs:
- new_global: float32 [3072, 1024], P('fsdp')
- new_momentum: float32 [16, 64, 3, 1024], P('fsdp', 'rep')
The draws below stay inside these ranges and needn't reach their ends.
Inputs may be any that keep to these rules, and one draw needn't show every extreme that they name: `norm_gain`: positive gains.
All inputs are finite; a program needn't handle non-finite values.
Results may differ from the reference program's by a relative error of at most 0.005.
Values may be sent and summed in bfloat16 or wider, within the bound.
A program may use at most 32 MiB of HBM per device.

```python
import jax
import jax.numpy as jnp
from jax import lax

D = 3072
KVH = 8
HD = 128
TOK_DEV = 128
C = 1024
TOKENS = 131072
ROWS_OWN = 3
N_REP = 64
N_FSDP = 16


def draw_norm_gain(key, part):
    key = jax.random.fold_in(key, 17)
    position = jnp.arange(D, dtype=jnp.float32) / D
    rough = jax.random.uniform(key, (D,), jnp.float32, -0.35, 0.35)
    return jnp.exp2(1.6 * position) * jnp.exp(rough)


def draw_cotangent(key, part):
    key = jax.random.fold_in(key, 29)
    level_key, value_key = jax.random.split(key)
    group_rows = TOK_DEV * N_FSDP
    order = jax.random.permutation(level_key, N_REP).astype(jnp.float32)
    share = order / (N_REP - 1)
    shrink = 0.99 * group_rows ** (-0.5)
    level = jnp.exp2(-3.0 + 4.0 * share)
    values = jnp.clip(jax.random.normal(value_key, (N_REP, group_rows, C), jnp.float32), -3.0, 3.0)
    return (values * level[:, None, None] * shrink).reshape(N_REP * group_rows, C).astype(jnp.bfloat16)


def place_ends(values, rng, smallest, high):
    index_at = [jax.random.randint(jax.random.fold_in(rng, axis), (), 0, length) for axis, length in enumerate(values.shape)]
    main_axis = values.shape.index(max(values.shape))
    beside = index_at[:main_axis] + [(index_at[main_axis] + 1) % values.shape[main_axis]] + index_at[main_axis + 1:]
    return values.at[tuple(index_at)].set(smallest).at[tuple(beside)].set(high)


def block_levels(own_key, shape, cuts, low, top_value):
    loudness, own = 1.0, jax.random.fold_in(own_key, 6)
    for axis_at, parts in cuts:
        steps = jnp.exp(jax.random.uniform(jax.random.fold_in(own, axis_at), (parts,), jnp.float32, low / len(cuts), top_value / len(cuts)))
        loudness = loudness * jnp.repeat(steps, shape[axis_at] // parts).reshape([-1 if axis == axis_at else 1 for axis in range(len(shape))])
    return loudness


def centred(own_key, dims, scale, limit, cuts=(), kind=jnp.bfloat16):
    array = jax.random.normal(own_key, dims, jnp.float32) * scale
    if len(cuts) > 0:
        array = block_levels(own_key, dims, cuts, -0.22, 0.18) * array
    return jnp.clip(array, min=-limit, max=limit).astype(kind)


def setup_inputs(seed: int = 0) -> dict:
    streams_of = jax.random.split(jax.random.key(seed), 8)
    tokens = centred(streams_of[0], (TOKENS, D), 1.0, 6.0, ((0, 1024),))
    cotangent = draw_cotangent(jax.random.fold_in(streams_of[7], 71), 0)
    norm_gain = draw_norm_gain(jax.random.fold_in(streams_of[7], 71), 0)
    replica_drift = centred(streams_of[3], (N_REP, D, C), 0.5, 3.0, ((0, 64), (1, 16)), jnp.float32)
    exponents = place_ends(jax.random.randint(streams_of[4], (N_REP, D, KVH), 1, 4), jax.random.fold_in(streams_of[4], 1), 1, 3).astype(jnp.int32)
    global_weight = centred(streams_of[5], (D, C), 1.0, 6.0, ((0, 16),), jnp.float32)
    momentum = centred(streams_of[6], (N_FSDP, N_REP, ROWS_OWN, C), 0.5, 3.0, ((0, 16), (1, 64)), jnp.float32)
    return {"tokens": tokens, "cotangent": cotangent, "norm_gain": norm_gain, "replica_drift": replica_drift, "exponents": exponents, "global_weight": global_weight, "momentum": momentum}


inner_rate = 0.5
outer_rate = 0.7
momentum_decay = 0.9
code_limit = 7.0

def sylvester(length):
    row_index = jnp.arange(length, dtype=jnp.int32)[:, None]
    col_index = jnp.arange(length, dtype=jnp.int32)[None, :]
    parity = jnp.zeros((length, length), jnp.int32)
    for bit_pos in range(length.bit_length() - 1):
        parity = parity + (jnp.right_shift(row_index, bit_pos) & jnp.right_shift(col_index, bit_pos) & 1)
    return jnp.where(parity % 2 == 0, 1.0, -1.0).astype(jnp.float32)

def reference(tokens, cotangent, norm_gain, replica_drift, exponents, global_weight, momentum):
    sign_table = sylvester(HD)
    unit_scale = HD ** (-0.5)
    inputs = tokens.reshape(N_REP, N_FSDP, TOK_DEV, D)
    grads_in = cotangent.reshape(N_REP, N_FSDP, TOK_DEV, C)

    def replica(running, pieces):
        rep_tokens, rep_cots, rep_drift, rep_expo = pieces
        widened = rep_tokens.astype(jnp.float32)
        mean_square = lax.optimization_barrier(jnp.mean(widened * widened, axis=-1, keepdims=True))
        normed = (widened * lax.rsqrt(mean_square + 1e-06) * norm_gain).astype(jnp.bfloat16)

        def accumulate(gradient, group):
            group_rows, group_cots = group
            partial_value = lax.dot_general(group_rows, group_cots, (((0,), (0,)), ((), ())), preferred_element_type=jnp.float32)
            partial_value = lax.optimization_barrier(partial_value.astype(jnp.bfloat16))
            return (gradient + partial_value.astype(jnp.float32), None)
        gradient, _ = lax.scan(accumulate, jnp.zeros((D, C), jnp.float32), (normed, rep_cots))
        square = jnp.sum(gradient * gradient)
        factor = jnp.minimum(1.0, 1.0 / jnp.sqrt(square / (D * C) + 1e-06))
        pseudo_grad = rep_drift + inner_rate * factor * gradient
        blocks = pseudo_grad.reshape(D, KVH, HD)
        turned = jnp.einsum('dkh,hj->dkj', blocks, sign_table, precision=lax.Precision.HIGHEST) * unit_scale
        expo_float = rep_expo.astype(jnp.float32)
        code_vals = jnp.clip(turned * jnp.exp2(expo_float)[..., None], -code_limit, code_limit).astype(jnp.bfloat16)
        down_scale = jnp.exp2(-expo_float).astype(jnp.bfloat16)
        unrotated = jnp.einsum('dkh,hj->dkj', code_vals.astype(jnp.float32), sign_table, precision=lax.Precision.HIGHEST)
        decoded = unrotated * unit_scale * down_scale.astype(jnp.float32)[..., None]
        return (running + decoded.reshape(D, C), None)
    summed, _ = lax.scan(replica, jnp.zeros((D, C), jnp.float32), (inputs, grads_in, replica_drift, exponents))
    mean_delta = summed / N_REP
    new_momentum = momentum_decay * momentum.reshape(D, C) + mean_delta
    new_global = global_weight - outer_rate * (mean_delta + momentum_decay * new_momentum)
    return (new_global, new_momentum.reshape(N_FSDP, N_REP, ROWS_OWN, C))
```

```python
import functools

import jax
import jax.numpy as jnp
from jax import lax
from jax.experimental import pallas as pl
from jax.experimental.pallas import tpu as pltpu
from jax.sharding import PartitionSpec as P

inner_rate = 0.5
outer_rate = 0.7
momentum_decay = 0.9
code_limit = 7.0

BF16, F32 = jnp.bfloat16, jnp.float32
D, C, KVH, HD, TOK = 3072, 1024, 8, 128, 128
NXH, NZ, NCORE = 4, 8, 2
NY, NX = 8, 2
N_REP, N_FSDP, CHIPS = NXH * NZ * NCORE, NY * NX, NXH * NZ
ROWS = D // N_FSDP
OWN = ROWS // N_REP
BLK = OWN * KVH
FAR = NY // 2
PARTS = 4
HALF = PARTS // 2
CW = C // PARTS
GROUPS = 2 * FAR - 1
UNIT = HD ** (-0.5)


def hadamard():
    i = lax.broadcasted_iota(jnp.int32, (HD, HD), 0)
    j = lax.broadcasted_iota(jnp.int32, (HD, HD), 1)
    v = i & j
    for shift in (4, 2, 1):
        v = v ^ jnp.right_shift(v, shift)
    return jnp.where((v & 1) == 0, 1.0, -1.0).astype(BF16)


def rotate(v, signs):
    hi = v.astype(BF16)
    rest = v - hi.astype(F32)
    mid = rest.astype(BF16)
    low = (rest - mid.astype(F32)).astype(BF16)
    dot = functools.partial(jnp.dot, preferred_element_type=F32)
    return dot(hi, signs) + (dot(mid, signs) + dot(low, signs))


def kernel(tok, cot, gain, drift, expo, mom, upd_out, delta_out,
           nt, lhs, cot2, y_out, y_in, grad, base, limit, squares, codes, code_out, code_in, own_sum, sib_sum, upd,
           x_ss, x_rs, y_ss, y_rs, q_ss, q_rs, c_ss, c_rs, s_ss, s_rs, a_ss, a_rs, b_ss, b_rs, h_ss, h_rs):
    rep, f = lax.axis_index("rep"), lax.axis_index("fsdp")
    core = lax.rem(rep, NCORE)
    chip = rep // NCORE
    z, xh = lax.rem(chip, NZ), chip // NZ
    y, x = f // NX, lax.rem(f, NX)

    def rep_of(xh_, z_, core_):
        return (xh_ * NZ + z_) * NCORE + core_

    def at(rep_, f_):
        return {"rep": rep_, "fsdp": f_}

    def remote(src, dst, ss, rs, device):
        return pltpu.make_async_remote_copy(src_ref=src, dst_ref=dst, send_sem=ss, recv_sem=rs, device_id=device,
                                            device_id_type=pl.DeviceIdType.MESH)

    barrier = pltpu.get_barrier_semaphore()

    def greet_f(i, carry):
        pl.semaphore_signal(barrier, inc=1, device_id=at(rep, lax.rem(f + i, N_FSDP)), device_id_type=pl.DeviceIdType.MESH)
        return carry

    def greet_r(i, carry):
        pl.semaphore_signal(barrier, inc=1, device_id=at(lax.rem(rep + NCORE * i, N_REP), f),
                            device_id_type=pl.DeviceIdType.MESH)
        return carry

    lax.fori_loop(1, N_FSDP, greet_f, 0)
    lax.fori_loop(1, CHIPS, greet_r, 0)
    sibling = at(rep_of(xh, z, 1 - core), f)
    pl.semaphore_signal(barrier, inc=1, device_id=sibling, device_id_type=pl.DeviceIdType.MESH)

    wide = tok[...].astype(F32)
    scale = lax.rsqrt(jnp.mean(wide * wide, axis=-1, keepdims=True) + 1e-06)
    for b in range(D // HD):
        cols = slice(b * HD, (b + 1) * HD)
        block = tok[:, cols].astype(F32) * scale * gain[:, cols]
        nt[cols, :] = block.T.astype(BF16)

    pl.semaphore_wait(barrier, N_FSDP - 1 + CHIPS - 1 + 1)

    partner = at(rep, f + 1 - 2 * x)

    def cot_copy(p):
        return remote(cot.at[:, p * CW:(p + 1) * CW], cot2.at[p, TOK:, :], x_ss.at[p], x_rs.at[p], partner)

    def nt_rows(yy, xx):
        return pl.ds(pl.multiple_of((yy * NX + xx) * ROWS, ROWS), ROWS)

    def nt_copy(yy):
        return remote(nt.at[nt_rows(yy, 1 - x), :], lhs.at[yy, :, TOK:], x_ss.at[PARTS + yy], x_rs.at[PARTS + yy], partner)

    def dest(dist):
        return lax.rem(y + dist + NY, NY)

    order = [FAR] + [s * d for d in range(FAR - 1, 0, -1) for s in (1, -1)] + [0]
    sequence = [("c", 0), ("n", order[0]), ("c", HALF)]
    sequence += [("c", p) for p in range(PARTS) if p not in (0, HALF)]
    sequence += [("n", dist) for dist in order[1:]]
    for kind, which in sequence:
        (cot_copy(which) if kind == "c" else nt_copy(dest(which))).start()

    for p in range(PARTS):
        cot2[p, :TOK, :] = cot[:, p * CW:(p + 1) * CW]
    for yy in range(NY):
        lhs[yy, :, :TOK] = nt[nt_rows(yy, x), :]

    signs = hadamard()

    def y_copy(way, g, pp):
        return remote(y_out.at[way, g, pp], y_in.at[way, g, pp], y_ss.at[way, g, pp], y_rs.at[way, g, pp],
                      at(rep, dest(1 - 2 * way) * NX + x))

    def part_of(way, g, pp):
        return lax.rem(g + way, 2) * HALF + pp

    def partial_sum(yy, p):
        return jnp.dot(lhs[yy], cot2[p], preferred_element_type=F32)

    def y_send(g, ways, pps, ready):
        dist = FAR - (g + 1) // 2
        for pp in pps:
            for way in ways:
                value = partial_sum(dest((1 - 2 * way) * dist), part_of(way, g, pp))
                if ready:
                    y_copy(way, g - 2, pp).wait_recv()
                    value = value + y_in[way, g - 2, pp].astype(F32)
                y_out[way, g, pp] = value.astype(BF16)
                y_copy(way, g, pp).start()

    nt_copy(dest(FAR)).wait_recv()
    for pp in range(HALF):
        for way in range(2):
            cot_copy(way * HALF + pp).wait_recv()
            y_send(0, (way,), (pp,), False)
    for way in range(2):
        nt_copy(dest((1 - 2 * way) * (FAR - 1))).wait_recv()
    y_send(1, (0, 1), range(HALF), False)

    for k in range(KVH):
        cols = slice(k * HD, (k + 1) * HD)
        base[:, cols] = rotate(drift[0, :, cols], signs) * UNIT
        e = expo[0, :, k:k + 1].astype(F32)
        limit[:, cols] = jnp.broadcast_to(code_limit * jnp.exp2(-e), (ROWS, HD))

    y_send(2, (0, 1), range(HALF), True)
    for dist in order[3:]:
        nt_copy(dest(dist)).wait_recv()

    def y_step(g, carry):
        y_send(g, (0, 1), range(HALF), True)
        return carry

    lax.fori_loop(3, GROUPS, y_step, 0)

    total = jnp.zeros((8, CW), F32)
    for p in range(PARTS):
        value = partial_sum(y, p)
        for way in range(2):
            g = GROUPS - 1 if p // HALF == way else GROUPS - 2
            y_copy(way, g, p % HALF).wait_recv()
            value = value + y_in[way, g, p % HALF].astype(F32)
        grad[:, p * CW:(p + 1) * CW] = value
        total = total + jnp.sum((value * value).reshape(ROWS // 8, 8, CW), axis=0)
    mine = total[:, :HD]
    for i in range(1, CW // HD):
        mine = mine + total[:, i * HD:(i + 1) * HD]
    squares[f] = mine

    def q_copy(slot, ff):
        return remote(squares.at[slot], squares.at[slot], q_ss.at[ff], q_rs.at[slot], at(rep, ff))

    def q_start(i, carry):
        ff = lax.rem(f + i, N_FSDP)
        q_copy(f, ff).start()
        return carry

    lax.fori_loop(1, N_FSDP, q_start, 0)
    for k in range(KVH):
        cols = slice(k * HD, (k + 1) * HD)
        grad[:, cols] = rotate(grad[:, cols], signs) * (UNIT * inner_rate)

    def q_wait(i, carry):
        q_copy(lax.rem(f + i, N_FSDP), lax.rem(f + i, N_FSDP)).wait_recv()
        return carry

    lax.fori_loop(1, N_FSDP, q_wait, 0)
    square = jnp.sum(jnp.sum(squares[...], axis=0), keepdims=True)
    factor = jnp.minimum(1.0, 1.0 / jnp.sqrt(square * (1.0 / (D * C)) + 1e-06))

    for k in range(KVH):
        cols = slice(k * HD, (k + 1) * HD)
        bound = limit[:, cols]
        value = base[:, cols] + factor * grad[:, cols]
        codes[pl.ds(k, ROWS, stride=KVH), :] = jnp.clip(value, -bound, bound)
    code_out[...] = codes[...].reshape(CHIPS, NCORE * BLK, HD).astype(BF16)

    def c_copy(src, slot, there):
        return remote(code_out.at[src], code_in.at[slot], c_ss.at[src], c_rs.at[slot], at(there * NCORE + core, f))

    def other(i):
        return lax.rem(xh + i // NZ, NXH) * NZ + lax.rem(z + i, NZ)

    def c_start(i, carry):
        there = other(i)
        c_copy(there, chip, there).start()
        return carry

    lax.fori_loop(1, CHIPS, c_start, 0)
    code_in[chip] = code_out[chip]

    rows = [(j, k) for j in range(OWN) for k in range(KVH)]
    moved = jnp.concatenate([mom[0, 0, j:j + 1, k * HD:(k + 1) * HD] for j, k in rows], axis=0)

    def c_wait(i, carry):
        there = other(i)
        c_copy(there, there, there).wait_recv()
        return carry

    lax.fori_loop(1, CHIPS, c_wait, 0)
    summed = jnp.sum(code_in[...].astype(F32), axis=0)
    for c in range(NCORE):
        own_sum[c] = summed[c * BLK:(c + 1) * BLK]
    sib_copy = remote(own_sum.at[1 - core], sib_sum, s_ss.at[0], s_rs.at[0], sibling)
    sib_copy.start()
    sib_copy.wait_recv()
    mean_delta = rotate(own_sum[core] + sib_sum[...], signs) * (UNIT / N_REP)
    new_momentum = momentum_decay * moved + mean_delta
    upd[xh, z, core] = outer_rate * (mean_delta + momentum_decay * new_momentum)

    def a_copy(i, slot_z, slot_x, there_z, there_x, sem):
        return remote(upd.at[slot_x, slot_z, core], upd.at[slot_x, slot_z, core], a_ss.at[i], a_rs.at[sem],
                      at(rep_of(there_x, there_z, core), f))

    @pl.when(core == 0)
    def _():
        for i in range(1, NZ):
            a_copy(i, z, xh, lax.rem(z + i, NZ), xh, z).start()
        for i in range(1, NZ):
            zz = lax.rem(z + i, NZ)
            a_copy(i, zz, xh, zz, xh, zz).wait_recv()

        def line(i, row, there, sem):
            return remote(upd.at[row, :, 0], upd.at[row, :, 0], b_ss.at[i], b_rs.at[sem], at(rep_of(there, z, 0), f))

        def hand(row):
            return remote(upd.at[row, :, 0], upd.at[row, :, 0], h_ss.at[row], h_rs.at[row], sibling)

        for i in range(1, NXH):
            line(i, xh, lax.rem(xh + i, NXH), xh).start()
        hand(xh).start()
        for i in range(1, NXH):
            xx = lax.rem(xh + i, NXH)
            line(i, xx, xx, xx).wait_recv()
            hand(xx).start()
        for r in range(NZ):
            remote(upd.at[:, r, 1], upd.at[:, r, 1], h_ss.at[r], h_rs.at[r], sibling).wait_recv()
        for r in range(NXH):
            hand(r).wait_send()
        for i in range(1, NXH):
            line(i, xh, xh, xh).wait_send()
        for i in range(1, NZ):
            a_copy(i, z, xh, z, xh, z).wait_send()

    @pl.when(core == 1)
    def _():
        for i in range(1, NXH):
            a_copy(i, z, xh, z, lax.rem(xh + i, NXH), xh).start()
        for i in range(1, NXH):
            xx = lax.rem(xh + i, NXH)
            a_copy(i, z, xx, z, xx, xx).wait_recv()

        def line(i, row, there, sem):
            return remote(upd.at[:, row, 1], upd.at[:, row, 1], b_ss.at[i], b_rs.at[sem], at(rep_of(xh, there, 1), f))

        def hand(row):
            return remote(upd.at[:, row, 1], upd.at[:, row, 1], h_ss.at[row], h_rs.at[row], sibling)

        for i in range(1, NZ):
            line(i, z, lax.rem(z + i, NZ), z).start()
        hand(z).start()
        for i in range(1, NZ):
            zz = lax.rem(z + i, NZ)
            line(i, zz, zz, zz).wait_recv()
            hand(zz).start()
        for r in range(NXH):
            remote(upd.at[r, :, 0], upd.at[r, :, 0], h_ss.at[r], h_rs.at[r], sibling).wait_recv()
        for r in range(NZ):
            hand(r).wait_send()
        for i in range(1, NZ):
            line(i, z, z, z).wait_send()
        for i in range(1, NXH):
            a_copy(i, z, xh, z, xh, xh).wait_send()

    flat = upd.reshape(ROWS * KVH, HD)
    for k in range(KVH):
        upd_out[:, k * HD:(k + 1) * HD] = flat[pl.ds(k, ROWS, stride=KVH), :]
    for i, (j, k) in enumerate(rows):
        delta_out[j:j + 1, k * HD:(k + 1) * HD] = mean_delta[i:i + 1, :]

    for p in range(PARTS):
        cot_copy(p).wait_send()
    for yy in range(NY):
        nt_copy(yy).wait_send()

    def y_drain(g, carry):
        for way in range(2):
            for pp in range(HALF):
                y_copy(way, g, pp).wait_send()
        return carry

    lax.fori_loop(0, GROUPS, y_drain, 0)

    def q_drain(i, carry):
        q_copy(f, lax.rem(f + i, N_FSDP)).wait_send()
        return carry

    lax.fori_loop(1, N_FSDP, q_drain, 0)

    def c_drain(i, carry):
        there = other(i)
        c_copy(there, chip, there).wait_send()
        return carry

    lax.fori_loop(1, CHIPS, c_drain, 0)
    sib_copy.wait_send()


def body(tokens, cotangent, norm_gain, replica_drift, exponents, global_weight, momentum):
    dma = pltpu.SemaphoreType.DMA
    vmem = pl.BlockSpec(memory_space=pltpu.VMEM)
    update, mean_delta = pl.pallas_call(
        kernel,
        out_shape=(jax.ShapeDtypeStruct((ROWS, C), F32), jax.ShapeDtypeStruct((OWN, C), F32)),
        in_specs=[vmem] * 6,
        out_specs=(vmem, vmem),
        scratch_shapes=[
            pltpu.VMEM((D, TOK), BF16),
            pltpu.VMEM((NY, ROWS, NX * TOK), BF16),
            pltpu.VMEM((PARTS, NX * TOK, CW), BF16),
            pltpu.VMEM((2, GROUPS, HALF, ROWS, CW), BF16),
            pltpu.VMEM((2, GROUPS, HALF, ROWS, CW), BF16),
            pltpu.VMEM((ROWS, C), F32),
            pltpu.VMEM((ROWS, C), F32),
            pltpu.VMEM((ROWS, C), F32),
            pltpu.VMEM((N_FSDP, 8, HD), F32),
            pltpu.VMEM((ROWS * KVH, HD), F32),
            pltpu.VMEM((CHIPS, NCORE * BLK, HD), BF16),
            pltpu.VMEM((CHIPS, NCORE * BLK, HD), BF16),
            pltpu.VMEM((NCORE, BLK, HD), F32),
            pltpu.VMEM((BLK, HD), F32),
            pltpu.VMEM((NXH, NZ, NCORE, BLK, HD), F32),
            dma((PARTS + NY,)), dma((PARTS + NY,)),
            dma((2, GROUPS, HALF)), dma((2, GROUPS, HALF)),
            dma((N_FSDP,)), dma((N_FSDP,)),
            dma((CHIPS,)), dma((CHIPS,)),
            dma((1,)), dma((1,)),
            dma((NZ,)), dma((NZ,)),
            dma((NZ,)), dma((NZ,)),
            dma((NZ,)), dma((NZ,)),
        ],
        compiler_params=pltpu.CompilerParams(collective_id=0, has_side_effects=True, vmem_limit_bytes=48 * 1024 * 1024),
        cost_estimate=pl.CostEstimate(flops=2 * TOK * D * C, bytes_accessed=4 * 1024 * 1024, transcendentals=0),
    )(tokens, cotangent, norm_gain.reshape(1, D), replica_drift, exponents, momentum)
    new_global = global_weight - update
    new_momentum = momentum_decay * momentum + mean_delta.reshape(momentum.shape)
    return new_global, new_momentum


def solution(mesh):
    placed = (
        P(("rep", "fsdp"), None),
        P(("rep", "fsdp"), None),
        P(),
        P("rep", "fsdp", None),
        P("rep", "fsdp", None),
        P("fsdp", None),
        P("fsdp", "rep", None, None),
    )
    return jax.shard_map(
        body,
        mesh=mesh,
        in_specs=placed,
        out_specs=(P("fsdp", None), P("fsdp", "rep", None, None)),
        check_vma=False,
    )
```

```python
import functools

import jax
import jax.numpy as jnp
from jax import lax
from jax.experimental import pallas as pl
from jax.experimental.pallas import tpu as pltpu
from jax.sharding import PartitionSpec as P

inner_rate = 0.5
outer_rate = 0.7
momentum_decay = 0.9
code_limit = 7.0

BF16, F32 = jnp.bfloat16, jnp.float32
D, C, KVH, HD, TOK = 3072, 1024, 8, 128, 128
NXH, NZ, NCORE = 4, 8, 2
NY, NX = 8, 2
N_REP, N_FSDP, CHIPS = NXH * NZ * NCORE, NY * NX, NXH * NZ
ROWS = D // N_FSDP
OWN = ROWS // N_REP
BLK = OWN * KVH
FAR = NY // 2
PARTS = 4
HALF = ROWS // 2
CW = C // PARTS
GROUPS = 2 * FAR - 1
UNIT = HD ** (-0.5)
ENCODE_MIB, COMBINE_MIB = 60, 60


def hadamard():
    i = lax.broadcasted_iota(jnp.int32, (HD, HD), 0)
    j = lax.broadcasted_iota(jnp.int32, (HD, HD), 1)
    v = i & j
    for shift in (4, 2, 1):
        v = v ^ jnp.right_shift(v, shift)
    return jnp.where((v & 1) == 0, 1.0, -1.0).astype(BF16)


def split(v):
    hi = v.astype(BF16)
    rest = v - hi.astype(F32)
    mid = rest.astype(BF16)
    return hi, mid, (rest - mid.astype(F32)).astype(BF16)


def rotate(v, signs, terms):
    parts = split(v)[:terms]
    return jnp.dot(jnp.concatenate(parts, axis=1), jnp.concatenate([signs] * terms, axis=0), preferred_element_type=F32)


def place():
    rep, f = lax.axis_index("rep"), lax.axis_index("fsdp")
    chip = rep // NCORE
    return rep, f, lax.rem(rep, NCORE), chip, lax.rem(chip, NZ), chip // NZ


def at(rep, f):
    return {"rep": rep, "fsdp": f}


def remote(src, dst, ss, rs, device):
    return pltpu.make_async_remote_copy(src_ref=src, dst_ref=dst, send_sem=ss, recv_sem=rs, device_id=device,
                                        device_id_type=pl.DeviceIdType.MESH)


def greet(barrier, device):
    pl.semaphore_signal(barrier, inc=1, device_id=device, device_id_type=pl.DeviceIdType.MESH)


def encode(tok_hbm, cot, gain_hbm, drift_hbm, expo_hbm, code_out,
           tok, gain, drift, expo, l_s, nt, lhs, cot2, y_out, y_in, grad, base, limit, squares, codes,
           x_ss, x_rs, y_ss, y_rs, q_ss, q_rs):
    rep, f, _, _, _, _ = place()
    y, x = f // NX, lax.rem(f, NX)

    def cot_load(p):
        return pltpu.make_async_copy(cot.at[:, p * CW:(p + 1) * CW], cot2.at[p, :TOK, :], l_s.at[p])

    loads = [pltpu.make_async_copy(src, dst, l_s.at[PARTS + i]) for i, (src, dst) in enumerate(
        ((tok_hbm, tok), (gain_hbm, gain), (drift_hbm, drift), (expo_hbm, expo)))]
    loads[0].start()
    loads[1].start()
    for p in range(PARTS):
        cot_load(p).start()
    for load in loads[2:]:
        load.start()

    barrier = pltpu.get_barrier_semaphore()

    def greet_f(i, carry):
        greet(barrier, at(rep, lax.rem(f + i, N_FSDP)))
        return carry

    lax.fori_loop(1, N_FSDP, greet_f, 0)
    pl.semaphore_wait(barrier, N_FSDP - 1)

    partner = at(rep, f + 1 - 2 * x)

    def cot_copy(p):
        return remote(cot.at[:, p * CW:(p + 1) * CW], cot2.at[p, TOK:, :], x_ss.at[p], x_rs.at[p], partner)

    def nt_rows(yy, xx):
        return pl.ds(pl.multiple_of((yy * NX + xx) * ROWS, ROWS), ROWS)

    def nt_copy(yy):
        return remote(nt.at[nt_rows(yy, 1 - x), :], lhs.at[yy, :, TOK:], x_ss.at[PARTS + yy], x_rs.at[PARTS + yy], partner)

    def dest(dist):
        return lax.rem(y + dist + NY, NY)

    cot_copy(0).start()
    cot_copy(1).start()

    loads[0].wait()
    loads[1].wait()
    wide = tok[...].astype(F32)
    scale = lax.rsqrt(jnp.mean(wide * wide, axis=-1, keepdims=True) + 1e-06)

    def norm_chunk(dist):
        yy = dest(dist)
        for b in range(NX * ROWS // HD):
            cols = pl.ds(pl.multiple_of(yy * (NX * ROWS) + b * HD, HD), HD)
            block = tok[:, cols].astype(F32) * scale * gain[:, cols]
            nt[cols, :] = block.T.astype(BF16)
        nt_copy(yy).start()
        lhs[yy, :, :TOK] = nt[nt_rows(yy, x), :]

    norm_chunk(FAR)
    for p in range(2, PARTS):
        cot_copy(p).start()
    norm_chunk(FAR - 1)
    norm_chunk(1 - FAR)

    signs = hadamard()

    def y_copy(way, g, p):
        return remote(y_out.at[way, g, p], y_in.at[way, g, p], y_ss.at[way], y_rs.at[way, g, p],
                      at(rep, dest(1 - 2 * way) * NX + x))

    def half_of(way, g):
        return pl.ds(pl.multiple_of(lax.rem(g + way, 2) * HALF, HALF), HALF)

    def y_send(g, p, ready):
        dist = FAR - (g + 1) // 2
        rows = [lhs[dest((1 - 2 * way) * dist), half_of(way, g), :] for way in range(2)]
        both = jnp.dot(jnp.concatenate(rows, axis=0), cot2[p], preferred_element_type=F32)
        for way in range(2):
            value = both[way * HALF:(way + 1) * HALF]
            if ready:
                y_copy(way, g - 2, p).wait_recv()
                value = value + y_in[way, g - 2, p].astype(F32)
            y_out[way, g, p] = value.astype(BF16)
            y_copy(way, g, p).start()

    for p in range(PARTS):
        cot_load(p).wait()
    nt_copy(dest(FAR)).wait_recv()
    for p in range(PARTS):
        cot_copy(p).wait_recv()
        y_send(0, p, False)
    norm_chunk(FAR - 2)
    norm_chunk(2 - FAR)
    for way in range(2):
        nt_copy(dest((1 - 2 * way) * (FAR - 1))).wait_recv()
    for p in range(PARTS):
        y_send(1, p, False)
    rest = [0] + [s * d for d in range(1, FAR - 2) for s in (1, -1)]
    for dist in rest[1:] + rest[:1]:
        norm_chunk(dist)
    for p in range(PARTS):
        y_send(2, p, True)

    for load in loads[2:]:
        load.wait()
    for k in range(KVH):
        cols = slice(k * HD, (k + 1) * HD)
        base[:, cols] = rotate(drift[0, :, cols], signs, 2) * UNIT
    head = lax.broadcasted_iota(jnp.int32, (KVH, C), 0) == lax.broadcasted_iota(jnp.int32, (KVH, C), 1) // HD
    bounds = (code_limit * jnp.exp2(-expo[...].astype(F32))).astype(BF16)
    limit[...] = lax.dot_general(bounds, head.astype(BF16), (((0,), (0,)), ((), ())), preferred_element_type=F32)

    for dist in [FAR - 2, 2 - FAR] + rest:
        nt_copy(dest(dist)).wait_recv()

    def y_step(g, carry):
        for p in range(PARTS):
            y_send(g, p, True)
        return carry

    lax.fori_loop(3, GROUPS, y_step, 0)

    total = jnp.zeros((8, CW), F32)
    for p in range(PARTS):
        cols = slice(p * CW, (p + 1) * CW)
        value = jnp.dot(lhs[y], cot2[p], preferred_element_type=F32)
        for way in range(2):
            y_copy(way, GROUPS - 2, p).wait_recv()
        early = [y_in[1 - half, GROUPS - 2, p].astype(F32) for half in range(2)]
        for half in range(2):
            rows = slice(half * HALF, (half + 1) * HALF)
            y_copy(half, GROUPS - 1, p).wait_recv()
            some = value[rows] + early[half] + y_in[half, GROUPS - 1, p].astype(F32)
            grad[rows, cols] = some
            total = total + jnp.sum((some * some).reshape(HALF // 8, 8, CW), axis=0)
    mine = total[:, :HD]
    for i in range(1, CW // HD):
        mine = mine + total[:, i * HD:(i + 1) * HD]
    squares[f] = mine

    def q_start(i, carry):
        remote(squares.at[f], squares.at[f], q_ss.at[0], q_rs.at[0], at(rep, lax.rem(f + i, N_FSDP))).start()
        return carry

    lax.fori_loop(1, N_FSDP, q_start, 0)
    for k in range(KVH):
        cols = slice(k * HD, (k + 1) * HD)
        grad[:, cols] = rotate(grad[:, cols], signs, 2) * (UNIT * inner_rate)

    for p in range(PARTS):
        cot_copy(p).wait_send()
    for yy in range(NY):
        nt_copy(yy).wait_send()
    for way in range(2):
        remote(y_out.at[way], y_in.at[way], y_ss.at[way], y_rs.at[0, 0, 0], at(rep, dest(1 - 2 * way) * NX + x)).wait_send()
    others = pl.ds(0, N_FSDP - 1)
    all_squares = remote(squares.at[others], squares.at[others], q_ss.at[0], q_rs.at[0], at(rep, lax.rem(f + 1, N_FSDP)))
    all_squares.wait_send()
    all_squares.wait_recv()
    square = jnp.sum(jnp.sum(squares[...], axis=0), keepdims=True)
    factor = jnp.minimum(1.0, 1.0 / jnp.sqrt(square * (1.0 / (D * C)) + 1e-06))

    for k in range(KVH):
        cols = slice(k * HD, (k + 1) * HD)
        bound = limit[:, cols]
        codes[pl.ds(k, ROWS, stride=KVH), :] = jnp.clip(base[:, cols] + factor * grad[:, cols], -bound, bound)
    code_out[...] = codes[...].reshape(CHIPS, NCORE * BLK, HD).astype(BF16)


def combine(code_out, mom, upd_out, delta_out,
            code_in, own_sum, sib_sum, upd, c_ss, c_rs, s_ss, s_rs, a_ss, a_rs, b_ss, b_rs, h_ss, h_rs):
    rep, f, core, chip, z, xh = place()

    def rep_of(xh_, z_, core_):
        return (xh_ * NZ + z_) * NCORE + core_

    barrier = pltpu.get_barrier_semaphore()

    def greet_r(i, carry):
        greet(barrier, at(lax.rem(rep + NCORE * i, N_REP), f))
        return carry

    lax.fori_loop(1, CHIPS, greet_r, 0)
    sibling = at(rep_of(xh, z, 1 - core), f)
    greet(barrier, sibling)
    pl.semaphore_wait(barrier, CHIPS)

    def c_start(i, carry):
        there = lax.rem(xh + lax.rem(i // NZ + 2, NXH), NXH) * NZ + lax.rem(z + i, NZ)

        @pl.when(there != chip)
        def _():
            remote(code_out.at[there], code_in.at[chip], c_ss.at[0], c_rs.at[0], at(there * NCORE + core, f)).start()

        return carry

    lax.fori_loop(0, CHIPS, c_start, 0)
    own_code = pltpu.make_async_copy(code_out.at[chip], code_in.at[chip], s_ss.at[1])
    own_code.start()
    others = pl.ds(0, CHIPS - 1)
    all_codes = remote(code_out.at[others], code_in.at[others], c_ss.at[0], c_rs.at[0], sibling)
    own_code.wait()
    all_codes.wait_send()
    all_codes.wait_recv()
    summed = jnp.sum(code_in[...].astype(F32), axis=0)
    for c in range(NCORE):
        own_sum[c] = summed[c * BLK:(c + 1) * BLK]
    sib_copy = remote(own_sum.at[1 - core], sib_sum, s_ss.at[0], s_rs.at[0], sibling)
    sib_copy.start()
    sib_copy.wait()
    signs = hadamard()
    mean_delta = rotate(own_sum[core] + sib_sum[...], signs, 3) * (UNIT / N_REP)
    new_momentum = momentum_decay * mom[...] + mean_delta
    upd[xh, z, core] = outer_rate * (mean_delta + momentum_decay * new_momentum)

    def a_copy(i, slot_z, slot_x, there_z, there_x, sem):
        return remote(upd.at[slot_x, slot_z, core], upd.at[slot_x, slot_z, core], a_ss.at[i], a_rs.at[sem],
                      at(rep_of(there_x, there_z, core), f))

    @pl.when(core == 0)
    def _():
        for i in range(1, NZ):
            a_copy(i, z, xh, lax.rem(z + i, NZ), xh, z).start()
        for i in range(1, NZ):
            zz = lax.rem(z + i, NZ)
            a_copy(i, zz, xh, zz, xh, zz).wait_recv()

        def line(i, row, there, sem):
            return remote(upd.at[row, :, 0], upd.at[row, :, 0], b_ss.at[i], b_rs.at[sem], at(rep_of(there, z, 0), f))

        def hand(row):
            return remote(upd.at[row, :, 0], upd.at[row, :, 0], h_ss.at[row], h_rs.at[row], sibling)

        for i in range(1, NXH):
            line(i, xh, lax.rem(xh + i, NXH), xh).start()
        hand(xh).start()
        for i in range(1, NXH):
            xx = lax.rem(xh + i, NXH)
            line(i, xx, xx, xx).wait_recv()
            hand(xx).start()
        for r in range(NZ):
            remote(upd.at[:, r, 1], upd.at[:, r, 1], h_ss.at[r], h_rs.at[r], sibling).wait_recv()
        for r in range(NXH):
            hand(r).wait_send()
        for i in range(1, NXH):
            line(i, xh, xh, xh).wait_send()
        for i in range(1, NZ):
            a_copy(i, z, xh, z, xh, z).wait_send()

    @pl.when(core == 1)
    def _():
        for i in range(1, NXH):
            a_copy(i, z, xh, z, lax.rem(xh + i, NXH), xh).start()
        for i in range(1, NXH):
            xx = lax.rem(xh + i, NXH)
            a_copy(i, z, xx, z, xx, xx).wait_recv()

        def line(i, row, there, sem):
            return remote(upd.at[:, row, 1], upd.at[:, row, 1], b_ss.at[i], b_rs.at[sem], at(rep_of(xh, there, 1), f))

        def hand(row):
            return remote(upd.at[:, row, 1], upd.at[:, row, 1], h_ss.at[row], h_rs.at[row], sibling)

        for i in range(1, NZ):
            line(i, z, lax.rem(z + i, NZ), z).start()
        hand(z).start()
        for i in range(1, NZ):
            zz = lax.rem(z + i, NZ)
            line(i, zz, zz, zz).wait_recv()
            hand(zz).start()
        for r in range(NXH):
            remote(upd.at[r, :, 0], upd.at[r, :, 0], h_ss.at[r], h_rs.at[r], sibling).wait_recv()
        for r in range(NZ):
            hand(r).wait_send()
        for i in range(1, NZ):
            line(i, z, z, z).wait_send()
        for i in range(1, NXH):
            a_copy(i, z, xh, z, xh, xh).wait_send()

    flat = upd.reshape(ROWS * KVH, HD)
    for k in range(KVH):
        upd_out[:, k * HD:(k + 1) * HD] = flat[pl.ds(k, ROWS, stride=KVH), :]
    delta_out[...] = mean_delta


def body(tokens, cotangent, norm_gain, replica_drift, exponents, global_weight, momentum):
    dma = pltpu.SemaphoreType.DMA
    vmem = pl.BlockSpec(memory_space=pltpu.VMEM)
    hbm = pl.BlockSpec(memory_space=pl.ANY)
    own_rows = momentum.reshape(BLK, HD)
    codes = pl.pallas_call(
        encode,
        out_shape=jax.ShapeDtypeStruct((CHIPS, NCORE * BLK, HD), BF16),
        in_specs=[hbm] * 5,
        out_specs=vmem,
        scratch_shapes=[
            pltpu.VMEM((TOK, D), BF16),
            pltpu.VMEM((1, D), F32),
            pltpu.VMEM((1, ROWS, C), F32),
            pltpu.VMEM((KVH, ROWS), jnp.int32),
            dma((PARTS + 4,)),
            pltpu.VMEM((D, TOK), BF16),
            pltpu.VMEM((NY, ROWS, NX * TOK), BF16),
            pltpu.VMEM((PARTS, NX * TOK, CW), BF16),
            pltpu.VMEM((2, GROUPS, PARTS, HALF, CW), BF16),
            pltpu.VMEM((2, GROUPS, PARTS, HALF, CW), BF16),
            pltpu.VMEM((ROWS, C), F32),
            pltpu.VMEM((ROWS, C), F32),
            pltpu.VMEM((ROWS, C), F32),
            pltpu.VMEM((N_FSDP, 8, HD), F32),
            pltpu.VMEM((ROWS * KVH, HD), F32),
            dma((PARTS + NY,)), dma((PARTS + NY,)),
            dma((2,)), dma((2, GROUPS, PARTS)),
            dma((1,)), dma((1,)),
        ],
        compiler_params=pltpu.CompilerParams(collective_id=0, has_side_effects=True, vmem_limit_bytes=ENCODE_MIB * 2 ** 20),
        cost_estimate=pl.CostEstimate(flops=2 * TOK * D * C, bytes_accessed=4 * 1024 * 1024, transcendentals=0),
    )(tokens, cotangent, norm_gain.reshape(1, D), replica_drift, exponents[0].T)
    update, mean_delta = pl.pallas_call(
        combine,
        out_shape=(jax.ShapeDtypeStruct((ROWS, C), F32), jax.ShapeDtypeStruct((BLK, HD), F32)),
        in_specs=[hbm, vmem],
        out_specs=(vmem, vmem),
        scratch_shapes=[
            pltpu.VMEM((CHIPS, NCORE * BLK, HD), BF16),
            pltpu.VMEM((NCORE, BLK, HD), F32),
            pltpu.VMEM((BLK, HD), F32),
            pltpu.VMEM((NXH, NZ, NCORE, BLK, HD), F32),
            dma((1,)), dma((1,)),
            dma((2,)), dma((1,)),
            dma((NZ,)), dma((NZ,)),
            dma((NZ,)), dma((NZ,)),
            dma((NZ,)), dma((NZ,)),
        ],
        compiler_params=pltpu.CompilerParams(collective_id=1, has_side_effects=True, vmem_limit_bytes=COMBINE_MIB * 2 ** 20),
        cost_estimate=pl.CostEstimate(flops=2 * ROWS * C * HD, bytes_accessed=2 * 1024 * 1024, transcendentals=0),
    )(codes, own_rows)
    new_global = global_weight - update
    new_momentum = momentum_decay * own_rows + mean_delta
    return new_global, new_momentum.reshape(momentum.shape)


def solution(mesh):
    placed = (
        P(("rep", "fsdp"), None),
        P(("rep", "fsdp"), None),
        P(),
        P("rep", "fsdp", None),
        P("rep", "fsdp", None),
        P("fsdp", None),
        P("fsdp", "rep", None, None),
    )
    return jax.shard_map(
        body,
        mesh=mesh,
        in_specs=placed,
        out_specs=(P("fsdp", None), P("fsdp", "rep", None, None)),
        check_vma=False,
    )
```

```python
import functools

import jax
import jax.numpy as jnp
from jax import lax
from jax.experimental import pallas as pl
from jax.experimental.pallas import tpu as pltpu
from jax.sharding import PartitionSpec as P

inner_rate = 0.5
outer_rate = 0.7
momentum_decay = 0.9
code_limit = 7.0

BF16, F32 = jnp.bfloat16, jnp.float32
D, C, KVH, HD, TOK = 3072, 1024, 8, 128, 128
NXH, NZ, NCORE = 4, 8, 2
NY, NX = 8, 2
N_REP, N_FSDP, CHIPS = NXH * NZ * NCORE, NY * NX, NXH * NZ
ROWS = D // N_FSDP
OWN = ROWS // N_REP
BLK = OWN * KVH
FAR = NY // 2
PARTS = 4
HALF = ROWS // 2
CW = C // PARTS
GROUPS = 2 * FAR - 1
UNIT = HD ** (-0.5)
KERNEL_MIB = 60


def hadamard():
    i = lax.broadcasted_iota(jnp.int32, (HD, HD), 0)
    j = lax.broadcasted_iota(jnp.int32, (HD, HD), 1)
    v = i & j
    for shift in (4, 2, 1):
        v = v ^ jnp.right_shift(v, shift)
    return jnp.where((v & 1) == 0, 1.0, -1.0).astype(BF16)


def split(v):
    hi = v.astype(BF16)
    rest = v - hi.astype(F32)
    mid = rest.astype(BF16)
    return hi, mid, (rest - mid.astype(F32)).astype(BF16)


def rotate(v, signs, terms):
    parts = split(v)[:terms]
    return jnp.dot(jnp.concatenate(parts, axis=1), jnp.concatenate([signs] * terms, axis=0), preferred_element_type=F32)


def place():
    rep, f = lax.axis_index("rep"), lax.axis_index("fsdp")
    chip = rep // NCORE
    return rep, f, lax.rem(rep, NCORE), chip, lax.rem(chip, NZ), chip // NZ


def at(rep, f):
    return {"rep": rep, "fsdp": f}


def remote(src, dst, ss, rs, device):
    return pltpu.make_async_remote_copy(src_ref=src, dst_ref=dst, send_sem=ss, recv_sem=rs, device_id=device,
                                        device_id_type=pl.DeviceIdType.MESH)


def greet(barrier, device):
    pl.semaphore_signal(barrier, inc=1, device_id=device, device_id_type=pl.DeviceIdType.MESH)


def kernel(tok_hbm, cot, gain_hbm, drift_hbm, expo_hbm, mom_hbm, upd_out, delta_out,
           tok, gain, drift, expo, mom, l_s, nt, lhs, cot2, y_out, y_in, grad, base, limit, squares, codes,
           code_out, code_in, own_sum, sib_sum, upd,
           x_ss, x_rs, y_ss, y_rs, q_ss, q_rs, c_ss, c_rs, s_ss, s_rs, a_ss, a_rs, b_ss, b_rs, h_ss, h_rs):
    rep, f, core, chip, z, xh = place()
    y, x = f // NX, lax.rem(f, NX)

    def rep_of(xh_, z_, core_):
        return (xh_ * NZ + z_) * NCORE + core_

    sibling = at(rep_of(xh, z, 1 - core), f)

    def cot_load(p):
        return pltpu.make_async_copy(cot.at[:, p * CW:(p + 1) * CW], cot2.at[p, :TOK, :], l_s.at[p])

    loads = [pltpu.make_async_copy(src, dst, l_s.at[PARTS + i]) for i, (src, dst) in enumerate(
        ((tok_hbm, tok), (gain_hbm, gain), (drift_hbm, drift), (expo_hbm, expo), (mom_hbm, mom)))]
    loads[0].start()
    loads[1].start()
    for p in range(PARTS):
        cot_load(p).start()
    for load in loads[2:]:
        load.start()

    barrier = pltpu.get_barrier_semaphore()

    def greet_f(i, carry):
        greet(barrier, at(rep, lax.rem(f + i, N_FSDP)))
        return carry

    def greet_r(i, carry):
        greet(barrier, at(lax.rem(rep + NCORE * i, N_REP), f))
        return carry

    lax.fori_loop(1, N_FSDP, greet_f, 0)
    lax.fori_loop(1, CHIPS, greet_r, 0)
    greet(barrier, sibling)
    pl.semaphore_wait(barrier, N_FSDP - 1 + CHIPS)

    partner = at(rep, f + 1 - 2 * x)

    def cot_copy(p):
        return remote(cot.at[:, p * CW:(p + 1) * CW], cot2.at[p, TOK:, :], x_ss.at[p], x_rs.at[p], partner)

    def nt_rows(yy, xx):
        return pl.ds(pl.multiple_of((yy * NX + xx) * ROWS, ROWS), ROWS)

    def nt_copy(yy):
        return remote(nt.at[nt_rows(yy, 1 - x), :], lhs.at[yy, :, TOK:], x_ss.at[PARTS + yy], x_rs.at[PARTS + yy], partner)

    def dest(dist):
        return lax.rem(y + dist + NY, NY)

    cot_copy(0).start()
    cot_copy(1).start()

    loads[0].wait()
    loads[1].wait()
    wide = tok[...].astype(F32)
    scale = lax.rsqrt(jnp.mean(wide * wide, axis=-1, keepdims=True) + 1e-06)

    def norm_chunk(dist):
        yy = dest(dist)
        for b in range(NX * ROWS // HD):
            cols = pl.ds(pl.multiple_of(yy * (NX * ROWS) + b * HD, HD), HD)
            block = tok[:, cols].astype(F32) * scale * gain[:, cols]
            nt[cols, :] = block.T.astype(BF16)
        nt_copy(yy).start()
        lhs[yy, :, :TOK] = nt[nt_rows(yy, x), :]

    norm_chunk(FAR)
    for p in range(2, PARTS):
        cot_copy(p).start()
    norm_chunk(FAR - 1)
    norm_chunk(1 - FAR)

    signs = hadamard()

    def y_copy(way, g, p):
        return remote(y_out.at[way, g, p], y_in.at[way, g, p], y_ss.at[way], y_rs.at[way, g, p],
                      at(rep, dest(1 - 2 * way) * NX + x))

    def half_of(way, g):
        return pl.ds(pl.multiple_of(lax.rem(g + way, 2) * HALF, HALF), HALF)

    def y_send(g, p, ready):
        dist = FAR - (g + 1) // 2
        rows = [lhs[dest((1 - 2 * way) * dist), half_of(way, g), :] for way in range(2)]
        both = jnp.dot(jnp.concatenate(rows, axis=0), cot2[p], preferred_element_type=F32)
        for way in range(2):
            value = both[way * HALF:(way + 1) * HALF]
            if ready:
                y_copy(way, g - 2, p).wait_recv()
                value = value + y_in[way, g - 2, p].astype(F32)
            y_out[way, g, p] = value.astype(BF16)
            y_copy(way, g, p).start()

    for p in range(PARTS):
        cot_load(p).wait()
    nt_copy(dest(FAR)).wait_recv()
    for p in range(PARTS):
        cot_copy(p).wait_recv()
        y_send(0, p, False)
    norm_chunk(FAR - 2)
    norm_chunk(2 - FAR)
    for way in range(2):
        nt_copy(dest((1 - 2 * way) * (FAR - 1))).wait_recv()
    for p in range(PARTS):
        y_send(1, p, False)
    rest = [0] + [s * d for d in range(1, FAR - 2) for s in (1, -1)]
    for dist in rest[1:] + rest[:1]:
        norm_chunk(dist)
    for p in range(PARTS):
        y_send(2, p, True)

    for load in loads[2:]:
        load.wait()
    for k in range(KVH):
        cols = slice(k * HD, (k + 1) * HD)
        base[:, cols] = rotate(drift[0, :, cols], signs, 2) * UNIT
    head = lax.broadcasted_iota(jnp.int32, (KVH, C), 0) == lax.broadcasted_iota(jnp.int32, (KVH, C), 1) // HD
    bounds = (code_limit * jnp.exp2(-expo[...].astype(F32))).astype(BF16)
    limit[...] = lax.dot_general(bounds, head.astype(BF16), (((0,), (0,)), ((), ())), preferred_element_type=F32)

    for dist in [FAR - 2, 2 - FAR] + rest:
        nt_copy(dest(dist)).wait_recv()

    def y_step(g, carry):
        for p in range(PARTS):
            y_send(g, p, True)
        return carry

    lax.fori_loop(3, GROUPS, y_step, 0)

    total = jnp.zeros((8, CW), F32)
    for p in range(PARTS):
        cols = slice(p * CW, (p + 1) * CW)
        value = jnp.dot(lhs[y], cot2[p], preferred_element_type=F32)
        for way in range(2):
            y_copy(way, GROUPS - 2, p).wait_recv()
        early = [y_in[1 - half, GROUPS - 2, p].astype(F32) for half in range(2)]
        for half in range(2):
            rows = slice(half * HALF, (half + 1) * HALF)
            y_copy(half, GROUPS - 1, p).wait_recv()
            some = value[rows] + early[half] + y_in[half, GROUPS - 1, p].astype(F32)
            grad[rows, cols] = some
            total = total + jnp.sum((some * some).reshape(HALF // 8, 8, CW), axis=0)
    mine = total[:, :HD]
    for i in range(1, CW // HD):
        mine = mine + total[:, i * HD:(i + 1) * HD]
    squares[f] = mine

    def q_start(i, carry):
        remote(squares.at[f], squares.at[f], q_ss.at[0], q_rs.at[0], at(rep, lax.rem(f + i, N_FSDP))).start()
        return carry

    lax.fori_loop(1, N_FSDP, q_start, 0)
    for k in range(KVH):
        cols = slice(k * HD, (k + 1) * HD)
        grad[:, cols] = rotate(grad[:, cols], signs, 2) * (UNIT * inner_rate)

    for p in range(PARTS):
        cot_copy(p).wait_send()
    for yy in range(NY):
        nt_copy(yy).wait_send()
    for way in range(2):
        remote(y_out.at[way], y_in.at[way], y_ss.at[way], y_rs.at[0, 0, 0], at(rep, dest(1 - 2 * way) * NX + x)).wait_send()
    others = pl.ds(0, N_FSDP - 1)
    all_squares = remote(squares.at[others], squares.at[others], q_ss.at[0], q_rs.at[0], at(rep, lax.rem(f + 1, N_FSDP)))
    all_squares.wait_send()
    all_squares.wait_recv()
    square = jnp.sum(jnp.sum(squares[...], axis=0), keepdims=True)
    factor = jnp.minimum(1.0, 1.0 / jnp.sqrt(square * (1.0 / (D * C)) + 1e-06))

    group_rows = ROWS // NXH
    for dx in (2, 3, 1, 0):
        xx = lax.rem(xh + dx, NXH)
        some = pl.ds(pl.multiple_of(xx * group_rows, group_rows), group_rows)
        for k in range(KVH):
            cols = slice(k * HD, (k + 1) * HD)
            bound = limit[some, cols]
            value = base[some, cols] + factor * grad[some, cols]
            codes[dx, pl.ds(k, group_rows, stride=KVH), :] = jnp.clip(value, -bound, bound)
        code_out[pl.ds(xx * NZ, NZ)] = codes[dx].reshape(NZ, NCORE * BLK, HD).astype(BF16)

        def c_start(i, carry):
            there = xx * NZ + lax.rem(z + i, NZ)
            remote(code_out.at[there], code_in.at[chip], c_ss.at[0], c_rs.at[0], at(there * NCORE + core, f)).start()
            return carry

        lax.fori_loop(0 if dx else 1, NZ, c_start, 0)
    code_in[chip] = code_out[chip]

    chips = pl.ds(0, CHIPS - 1)
    all_codes = remote(code_out.at[chips], code_in.at[chips], c_ss.at[0], c_rs.at[0], sibling)
    all_codes.wait_send()
    all_codes.wait_recv()
    summed = jnp.sum(code_in[...].astype(F32), axis=0)
    for c in range(NCORE):
        own_sum[c] = summed[c * BLK:(c + 1) * BLK]
    sib_copy = remote(own_sum.at[1 - core], sib_sum, s_ss.at[0], s_rs.at[0], sibling)
    sib_copy.start()
    sib_copy.wait()
    mean_delta = rotate(own_sum[core] + sib_sum[...], signs, 3) * (UNIT / N_REP)
    new_momentum = momentum_decay * mom[...] + mean_delta
    upd[xh, z, core] = outer_rate * (mean_delta + momentum_decay * new_momentum)

    def a_copy(i, slot_z, slot_x, there_z, there_x, sem):
        return remote(upd.at[slot_x, slot_z, core], upd.at[slot_x, slot_z, core], a_ss.at[i], a_rs.at[sem],
                      at(rep_of(there_x, there_z, core), f))

    @pl.when(core == 0)
    def _():
        for i in range(1, NZ):
            a_copy(i, z, xh, lax.rem(z + i, NZ), xh, z).start()
        for i in range(1, NZ):
            zz = lax.rem(z + i, NZ)
            a_copy(i, zz, xh, zz, xh, zz).wait_recv()

        def line(i, row, there, sem):
            return remote(upd.at[row, :, 0], upd.at[row, :, 0], b_ss.at[i], b_rs.at[sem], at(rep_of(there, z, 0), f))

        def hand(row):
            return remote(upd.at[row, :, 0], upd.at[row, :, 0], h_ss.at[row], h_rs.at[row], sibling)

        for i in range(1, NXH):
            line(i, xh, lax.rem(xh + i, NXH), xh).start()
        hand(xh).start()
        for i in range(1, NXH):
            xx = lax.rem(xh + i, NXH)
            line(i, xx, xx, xx).wait_recv()
            hand(xx).start()
        for r in range(NZ):
            remote(upd.at[:, r, 1], upd.at[:, r, 1], h_ss.at[r], h_rs.at[r], sibling).wait_recv()
        for r in range(NXH):
            hand(r).wait_send()
        for i in range(1, NXH):
            line(i, xh, xh, xh).wait_send()
        for i in range(1, NZ):
            a_copy(i, z, xh, z, xh, z).wait_send()

    @pl.when(core == 1)
    def _():
        for i in range(1, NXH):
            a_copy(i, z, xh, z, lax.rem(xh + i, NXH), xh).start()
        for i in range(1, NXH):
            xx = lax.rem(xh + i, NXH)
            a_copy(i, z, xx, z, xx, xx).wait_recv()

        def line(i, row, there, sem):
            return remote(upd.at[:, row, 1], upd.at[:, row, 1], b_ss.at[i], b_rs.at[sem], at(rep_of(xh, there, 1), f))

        def hand(row):
            return remote(upd.at[:, row, 1], upd.at[:, row, 1], h_ss.at[row], h_rs.at[row], sibling)

        for i in range(1, NZ):
            line(i, z, lax.rem(z + i, NZ), z).start()
        hand(z).start()
        for i in range(1, NZ):
            zz = lax.rem(z + i, NZ)
            line(i, zz, zz, zz).wait_recv()
            hand(zz).start()
        for r in range(NXH):
            remote(upd.at[r, :, 0], upd.at[r, :, 0], h_ss.at[r], h_rs.at[r], sibling).wait_recv()
        for r in range(NZ):
            hand(r).wait_send()
        for i in range(1, NZ):
            line(i, z, z, z).wait_send()
        for i in range(1, NXH):
            a_copy(i, z, xh, z, xh, xh).wait_send()

    flat = upd.reshape(ROWS * KVH, HD)
    for k in range(KVH):
        upd_out[:, k * HD:(k + 1) * HD] = flat[pl.ds(k, ROWS, stride=KVH), :]
    delta_out[...] = mean_delta


def body(tokens, cotangent, norm_gain, replica_drift, exponents, global_weight, momentum):
    dma = pltpu.SemaphoreType.DMA
    vmem = pl.BlockSpec(memory_space=pltpu.VMEM)
    hbm = pl.BlockSpec(memory_space=pl.ANY)
    own_rows = momentum.reshape(BLK, HD)
    update, mean_delta = pl.pallas_call(
        kernel,
        out_shape=(jax.ShapeDtypeStruct((ROWS, C), F32), jax.ShapeDtypeStruct((BLK, HD), F32)),
        in_specs=[hbm] * 6,
        out_specs=(vmem, vmem),
        scratch_shapes=[
            pltpu.VMEM((TOK, D), BF16),
            pltpu.VMEM((1, D), F32),
            pltpu.VMEM((1, ROWS, C), F32),
            pltpu.VMEM((KVH, ROWS), jnp.int32),
            pltpu.VMEM((BLK, HD), F32),
            dma((PARTS + 5,)),
            pltpu.VMEM((D, TOK), BF16),
            pltpu.VMEM((NY, ROWS, NX * TOK), BF16),
            pltpu.VMEM((PARTS, NX * TOK, CW), BF16),
            pltpu.VMEM((2, GROUPS, PARTS, HALF, CW), BF16),
            pltpu.VMEM((2, GROUPS, PARTS, HALF, CW), BF16),
            pltpu.VMEM((ROWS, C), F32),
            pltpu.VMEM((ROWS, C), F32),
            pltpu.VMEM((ROWS, C), F32),
            pltpu.VMEM((N_FSDP, 8, HD), F32),
            pltpu.VMEM((NXH, ROWS // NXH * KVH, HD), F32),
            pltpu.VMEM((CHIPS, NCORE * BLK, HD), BF16),
            pltpu.VMEM((CHIPS, NCORE * BLK, HD), BF16),
            pltpu.VMEM((NCORE, BLK, HD), F32),
            pltpu.VMEM((BLK, HD), F32),
            pltpu.VMEM((NXH, NZ, NCORE, BLK, HD), F32),
            dma((PARTS + NY,)), dma((PARTS + NY,)),
            dma((2,)), dma((2, GROUPS, PARTS)),
            dma((1,)), dma((1,)),
            dma((1,)), dma((1,)),
            dma((1,)), dma((1,)),
            dma((NZ,)), dma((NZ,)),
            dma((NZ,)), dma((NZ,)),
            dma((NZ,)), dma((NZ,)),
        ],
        compiler_params=pltpu.CompilerParams(collective_id=0, has_side_effects=True, vmem_limit_bytes=KERNEL_MIB * 2 ** 20),
        cost_estimate=pl.CostEstimate(flops=2 * TOK * D * C, bytes_accessed=4 * 1024 * 1024, transcendentals=0),
    )(tokens, cotangent, norm_gain.reshape(1, D), replica_drift, exponents[0].T, own_rows)
    new_global = global_weight - update
    new_momentum = momentum_decay * own_rows + mean_delta
    return new_global, new_momentum.reshape(momentum.shape)


def solution(mesh):
    placed = (
        P(("rep", "fsdp"), None),
        P(("rep", "fsdp"), None),
        P(),
        P("rep", "fsdp", None),
        P("rep", "fsdp", None),
        P("fsdp", None),
        P("fsdp", "rep", None, None),
    )
    return jax.shard_map(
        body,
        mesh=mesh,
        in_specs=placed,
        out_specs=(P("fsdp", None), P("fsdp", "rep", None, None)),
        check_vma=False,
    )
```

```python
import functools

import jax
import jax.numpy as jnp
from jax import lax
from jax.experimental import pallas as pl
from jax.experimental.pallas import tpu as pltpu
from jax.sharding import PartitionSpec as P

inner_rate = 0.5
outer_rate = 0.7
momentum_decay = 0.9
code_limit = 7.0

BF16, F32 = jnp.bfloat16, jnp.float32
D, C, KVH, HD, TOK = 3072, 1024, 8, 128, 128
NXH, NZ, NCORE = 4, 8, 2
NY, NX = 8, 2
N_REP, N_FSDP, CHIPS = NXH * NZ * NCORE, NY * NX, NXH * NZ
ROWS = D // N_FSDP
OWN = ROWS // N_REP
BLK = OWN * KVH
FAR = NY // 2
PARTS = 4
HALF = ROWS // 2
CW = C // PARTS
GROUPS = 2 * FAR - 1
UNIT = HD ** (-0.5)
KERNEL_MIB = 60


def hadamard():
    i = lax.broadcasted_iota(jnp.int32, (HD, HD), 0)
    j = lax.broadcasted_iota(jnp.int32, (HD, HD), 1)
    v = i & j
    for shift in (4, 2, 1):
        v = v ^ jnp.right_shift(v, shift)
    return jnp.where((v & 1) == 0, 1.0, -1.0).astype(BF16)


def split(v):
    hi = v.astype(BF16)
    rest = v - hi.astype(F32)
    mid = rest.astype(BF16)
    return hi, mid, (rest - mid.astype(F32)).astype(BF16)


def rotate(v, signs, terms):
    parts = split(v)[:terms]
    return jnp.dot(jnp.concatenate(parts, axis=1), jnp.concatenate([signs] * terms, axis=0), preferred_element_type=F32)


def place():
    rep, f = lax.axis_index("rep"), lax.axis_index("fsdp")
    chip = rep // NCORE
    return rep, f, lax.rem(rep, NCORE), chip, lax.rem(chip, NZ), chip // NZ


def at(rep, f):
    return {"rep": rep, "fsdp": f}


def remote(src, dst, ss, rs, device):
    return pltpu.make_async_remote_copy(src_ref=src, dst_ref=dst, send_sem=ss, recv_sem=rs, device_id=device,
                                        device_id_type=pl.DeviceIdType.MESH)


def greet(barrier, device):
    pl.semaphore_signal(barrier, inc=1, device_id=device, device_id_type=pl.DeviceIdType.MESH)


def kernel(tok_hbm, cot, gain_hbm, drift_hbm, expo_hbm, mom_hbm, weight_hbm, new_out, momentum_out,
           tok, gain, drift, expo, mom, weight, l_s, nt, lhs, cot2, y_out, y_in, grad, base, limit, squares, codes,
           code_out, code_in, own_sum, sib_sum, upd,
           x_ss, x_rs, y_ss, y_rs, q_ss, q_rs, c_ss, c_rs, s_ss, s_rs, a_ss, a_rs, b_ss, b_rs, h_ss, h_rs):
    rep, f, core, chip, z, xh = place()
    y, x = f // NX, lax.rem(f, NX)

    def rep_of(xh_, z_, core_):
        return (xh_ * NZ + z_) * NCORE + core_

    sibling = at(rep_of(xh, z, 1 - core), f)

    def cot_load(p):
        return pltpu.make_async_copy(cot.at[:, p * CW:(p + 1) * CW], cot2.at[p, :TOK, :], l_s.at[p])

    loads = [pltpu.make_async_copy(src, dst, l_s.at[PARTS + i]) for i, (src, dst) in enumerate(
        ((tok_hbm, tok), (gain_hbm, gain), (drift_hbm, drift), (expo_hbm, expo), (mom_hbm, mom), (weight_hbm, weight)))]
    loads[0].start()
    loads[1].start()
    for p in range(PARTS):
        cot_load(p).start()
    for load in loads[2:]:
        load.start()

    barrier = pltpu.get_barrier_semaphore()

    def greet_f(i, carry):
        greet(barrier, at(rep, lax.rem(f + i, N_FSDP)))
        return carry

    def greet_r(i, carry):
        greet(barrier, at(lax.rem(rep + NCORE * i, N_REP), f))
        return carry

    lax.fori_loop(1, N_FSDP, greet_f, 0)
    lax.fori_loop(1, CHIPS, greet_r, 0)
    greet(barrier, sibling)
    pl.semaphore_wait(barrier, N_FSDP - 1 + CHIPS)

    partner = at(rep, f + 1 - 2 * x)

    def cot_copy(p):
        return remote(cot.at[:, p * CW:(p + 1) * CW], cot2.at[p, TOK:, :], x_ss.at[p], x_rs.at[p], partner)

    def nt_rows(yy, xx):
        return pl.ds(pl.multiple_of((yy * NX + xx) * ROWS, ROWS), ROWS)

    def nt_copy(yy):
        return remote(nt.at[nt_rows(yy, 1 - x), :], lhs.at[yy, :, TOK:], x_ss.at[PARTS + yy], x_rs.at[PARTS + yy], partner)

    def dest(dist):
        return lax.rem(y + dist + NY, NY)

    cot_copy(0).start()
    cot_copy(1).start()

    loads[0].wait()
    loads[1].wait()
    wide = tok[...].astype(F32)
    scale = lax.rsqrt(jnp.mean(wide * wide, axis=-1, keepdims=True) + 1e-06)

    def norm_chunk(dist):
        yy = dest(dist)
        for b in range(NX * ROWS // HD):
            cols = pl.ds(pl.multiple_of(yy * (NX * ROWS) + b * HD, HD), HD)
            block = tok[:, cols].astype(F32) * scale * gain[:, cols]
            nt[cols, :] = block.T.astype(BF16)
        nt_copy(yy).start()
        lhs[yy, :, :TOK] = nt[nt_rows(yy, x), :]

    norm_chunk(FAR)
    for p in range(2, PARTS):
        cot_copy(p).start()
    norm_chunk(FAR - 1)
    norm_chunk(1 - FAR)

    signs = hadamard()

    def y_copy(way, g, p):
        return remote(y_out.at[way, g, p], y_in.at[way, g, p], y_ss.at[way], y_rs.at[way, g, p],
                      at(rep, dest(1 - 2 * way) * NX + x))

    def half_of(way, g):
        return pl.ds(pl.multiple_of(lax.rem(g + way, 2) * HALF, HALF), HALF)

    def y_send(g, p, ready):
        dist = FAR - (g + 1) // 2
        rows = [lhs[dest((1 - 2 * way) * dist), half_of(way, g), :] for way in range(2)]
        both = jnp.dot(jnp.concatenate(rows, axis=0), cot2[p], preferred_element_type=F32)
        for way in range(2):
            value = both[way * HALF:(way + 1) * HALF]
            if ready:
                y_copy(way, g - 2, p).wait_recv()
                value = value + y_in[way, g - 2, p].astype(F32)
            y_out[way, g, p] = value.astype(BF16)
            y_copy(way, g, p).start()

    for p in range(PARTS):
        cot_load(p).wait()
    nt_copy(dest(FAR)).wait_recv()
    for p in range(PARTS):
        cot_copy(p).wait_recv()
        y_send(0, p, False)
    norm_chunk(FAR - 2)
    norm_chunk(2 - FAR)
    for way in range(2):
        nt_copy(dest((1 - 2 * way) * (FAR - 1))).wait_recv()
    for p in range(PARTS):
        y_send(1, p, False)
    rest = [0] + [s * d for d in range(1, FAR - 2) for s in (1, -1)]
    for dist in rest[1:] + rest[:1]:
        norm_chunk(dist)
    for p in range(PARTS):
        y_send(2, p, True)

    for load in loads[2:]:
        load.wait()
    for k in range(KVH):
        cols = slice(k * HD, (k + 1) * HD)
        base[:, cols] = rotate(drift[0, :, cols], signs, 2) * UNIT
    head = lax.broadcasted_iota(jnp.int32, (KVH, C), 0) == lax.broadcasted_iota(jnp.int32, (KVH, C), 1) // HD
    bounds = (code_limit * jnp.exp2(-expo[...].astype(F32))).astype(BF16)
    limit[...] = lax.dot_general(bounds, head.astype(BF16), (((0,), (0,)), ((), ())), preferred_element_type=F32)

    for dist in [FAR - 2, 2 - FAR] + rest:
        nt_copy(dest(dist)).wait_recv()

    def y_step(g, carry):
        for p in range(PARTS):
            y_send(g, p, True)
        return carry

    lax.fori_loop(3, GROUPS, y_step, 0)

    total = jnp.zeros((8, CW), F32)
    for p in range(PARTS):
        cols = slice(p * CW, (p + 1) * CW)
        value = jnp.dot(lhs[y], cot2[p], preferred_element_type=F32)
        for way in range(2):
            y_copy(way, GROUPS - 2, p).wait_recv()
        early = [y_in[1 - half, GROUPS - 2, p].astype(F32) for half in range(2)]
        for half in range(2):
            rows = slice(half * HALF, (half + 1) * HALF)
            y_copy(half, GROUPS - 1, p).wait_recv()
            some = value[rows] + early[half] + y_in[half, GROUPS - 1, p].astype(F32)
            grad[rows, cols] = some
            total = total + jnp.sum((some * some).reshape(HALF // 8, 8, CW), axis=0)
    mine = total[:, :HD]
    for i in range(1, CW // HD):
        mine = mine + total[:, i * HD:(i + 1) * HD]
    squares[f] = mine

    def q_start(i, carry):
        remote(squares.at[f], squares.at[f], q_ss.at[0], q_rs.at[0], at(rep, lax.rem(f + i, N_FSDP))).start()
        return carry

    lax.fori_loop(1, N_FSDP, q_start, 0)
    for k in range(KVH):
        cols = slice(k * HD, (k + 1) * HD)
        grad[:, cols] = rotate(grad[:, cols], signs, 2) * (UNIT * inner_rate)

    for p in range(PARTS):
        cot_copy(p).wait_send()
    for yy in range(NY):
        nt_copy(yy).wait_send()
    for way in range(2):
        remote(y_out.at[way], y_in.at[way], y_ss.at[way], y_rs.at[0, 0, 0], at(rep, dest(1 - 2 * way) * NX + x)).wait_send()
    others = pl.ds(0, N_FSDP - 1)
    all_squares = remote(squares.at[others], squares.at[others], q_ss.at[0], q_rs.at[0], at(rep, lax.rem(f + 1, N_FSDP)))
    all_squares.wait_send()
    all_squares.wait_recv()
    square = jnp.sum(jnp.sum(squares[...], axis=0), keepdims=True)
    factor = jnp.minimum(1.0, 1.0 / jnp.sqrt(square * (1.0 / (D * C)) + 1e-06))

    group_rows = ROWS // NXH
    for dx in (2, 3, 1, 0):
        xx = lax.rem(xh + dx, NXH)
        some = pl.ds(pl.multiple_of(xx * group_rows, group_rows), group_rows)
        for k in range(KVH):
            cols = slice(k * HD, (k + 1) * HD)
            bound = limit[some, cols]
            value = base[some, cols] + factor * grad[some, cols]
            codes[dx, pl.ds(k, group_rows, stride=KVH), :] = jnp.clip(value, -bound, bound)
        code_out[pl.ds(xx * NZ, NZ)] = codes[dx].reshape(NZ, NCORE * BLK, HD).astype(BF16)

        def c_start(i, carry):
            there = xx * NZ + lax.rem(z + i, NZ)
            remote(code_out.at[there], code_in.at[chip], c_ss.at[0], c_rs.at[0], at(there * NCORE + core, f)).start()
            return carry

        lax.fori_loop(0 if dx else 1, NZ, c_start, 0)
    code_in[chip] = code_out[chip]

    chips = pl.ds(0, CHIPS - 1)
    all_codes = remote(code_out.at[chips], code_in.at[chips], c_ss.at[0], c_rs.at[0], sibling)
    all_codes.wait_send()
    all_codes.wait_recv()
    summed = jnp.sum(code_in[...].astype(F32), axis=0)
    for c in range(NCORE):
        own_sum[c] = summed[c * BLK:(c + 1) * BLK]
    sib_copy = remote(own_sum.at[1 - core], sib_sum, s_ss.at[0], s_rs.at[0], sibling)
    sib_copy.start()
    sib_copy.wait()
    mean_delta = rotate(own_sum[core] + sib_sum[...], signs, 3) * (UNIT / N_REP)
    new_momentum = momentum_decay * mom[...] + mean_delta
    upd[xh, z, core] = outer_rate * (mean_delta + momentum_decay * new_momentum)

    def a_copy(i, slot_z, slot_x, there_z, there_x, sem):
        return remote(upd.at[slot_x, slot_z, core], upd.at[slot_x, slot_z, core], a_ss.at[i], a_rs.at[sem],
                      at(rep_of(there_x, there_z, core), f))

    @pl.when(core == 0)
    def _():
        for i in range(1, NZ):
            a_copy(i, z, xh, lax.rem(z + i, NZ), xh, z).start()
        for i in range(1, NZ):
            zz = lax.rem(z + i, NZ)
            a_copy(i, zz, xh, zz, xh, zz).wait_recv()

        def line(i, row, there, sem):
            return remote(upd.at[row, :, 0], upd.at[row, :, 0], b_ss.at[i], b_rs.at[sem], at(rep_of(there, z, 0), f))

        def hand(row):
            return remote(upd.at[row, :, 0], upd.at[row, :, 0], h_ss.at[row], h_rs.at[row], sibling)

        for i in range(1, NXH):
            line(i, xh, lax.rem(xh + i, NXH), xh).start()
        hand(xh).start()
        for i in range(1, NXH):
            xx = lax.rem(xh + i, NXH)
            line(i, xx, xx, xx).wait_recv()
            hand(xx).start()
        for r in range(NZ):
            remote(upd.at[:, r, 1], upd.at[:, r, 1], h_ss.at[r], h_rs.at[r], sibling).wait_recv()
        for r in range(NXH):
            hand(r).wait_send()
        for i in range(1, NXH):
            line(i, xh, xh, xh).wait_send()
        for i in range(1, NZ):
            a_copy(i, z, xh, z, xh, z).wait_send()

    @pl.when(core == 1)
    def _():
        for i in range(1, NXH):
            a_copy(i, z, xh, z, lax.rem(xh + i, NXH), xh).start()
        for i in range(1, NXH):
            xx = lax.rem(xh + i, NXH)
            a_copy(i, z, xx, z, xx, xx).wait_recv()

        def line(i, row, there, sem):
            return remote(upd.at[:, row, 1], upd.at[:, row, 1], b_ss.at[i], b_rs.at[sem], at(rep_of(xh, there, 1), f))

        def hand(row):
            return remote(upd.at[:, row, 1], upd.at[:, row, 1], h_ss.at[row], h_rs.at[row], sibling)

        for i in range(1, NZ):
            line(i, z, lax.rem(z + i, NZ), z).start()
        hand(z).start()
        for i in range(1, NZ):
            zz = lax.rem(z + i, NZ)
            line(i, zz, zz, zz).wait_recv()
            hand(zz).start()
        for r in range(NXH):
            remote(upd.at[r, :, 0], upd.at[r, :, 0], h_ss.at[r], h_rs.at[r], sibling).wait_recv()
        for r in range(NZ):
            hand(r).wait_send()
        for i in range(1, NZ):
            line(i, z, z, z).wait_send()
        for i in range(1, NXH):
            a_copy(i, z, xh, z, xh, xh).wait_send()

    flat = upd.reshape(ROWS * KVH, HD)
    for k in range(KVH):
        cols = slice(k * HD, (k + 1) * HD)
        new_out[:, cols] = weight[:, cols] - flat[pl.ds(k, ROWS, stride=KVH), :]
    momentum_out[...] = new_momentum


def body(tokens, cotangent, norm_gain, replica_drift, exponents, global_weight, momentum):
    dma = pltpu.SemaphoreType.DMA
    vmem = pl.BlockSpec(memory_space=pltpu.VMEM)
    hbm = pl.BlockSpec(memory_space=pl.ANY)
    own_rows = momentum.reshape(BLK, HD)
    new_global, new_momentum = pl.pallas_call(
        kernel,
        out_shape=(jax.ShapeDtypeStruct((ROWS, C), F32), jax.ShapeDtypeStruct((BLK, HD), F32)),
        in_specs=[hbm] * 7,
        out_specs=(vmem, vmem),
        scratch_shapes=[
            pltpu.VMEM((TOK, D), BF16),
            pltpu.VMEM((1, D), F32),
            pltpu.VMEM((1, ROWS, C), F32),
            pltpu.VMEM((KVH, ROWS), jnp.int32),
            pltpu.VMEM((BLK, HD), F32),
            pltpu.VMEM((ROWS, C), F32),
            dma((PARTS + 6,)),
            pltpu.VMEM((D, TOK), BF16),
            pltpu.VMEM((NY, ROWS, NX * TOK), BF16),
            pltpu.VMEM((PARTS, NX * TOK, CW), BF16),
            pltpu.VMEM((2, GROUPS, PARTS, HALF, CW), BF16),
            pltpu.VMEM((2, GROUPS, PARTS, HALF, CW), BF16),
            pltpu.VMEM((ROWS, C), F32),
            pltpu.VMEM((ROWS, C), F32),
            pltpu.VMEM((ROWS, C), F32),
            pltpu.VMEM((N_FSDP, 8, HD), F32),
            pltpu.VMEM((NXH, ROWS // NXH * KVH, HD), F32),
            pltpu.VMEM((CHIPS, NCORE * BLK, HD), BF16),
            pltpu.VMEM((CHIPS, NCORE * BLK, HD), BF16),
            pltpu.VMEM((NCORE, BLK, HD), F32),
            pltpu.VMEM((BLK, HD), F32),
            pltpu.VMEM((NXH, NZ, NCORE, BLK, HD), F32),
            dma((PARTS + NY,)), dma((PARTS + NY,)),
            dma((2,)), dma((2, GROUPS, PARTS)),
            dma((1,)), dma((1,)),
            dma((1,)), dma((1,)),
            dma((1,)), dma((1,)),
            dma((NZ,)), dma((NZ,)),
            dma((NZ,)), dma((NZ,)),
            dma((NZ,)), dma((NZ,)),
        ],
        compiler_params=pltpu.CompilerParams(collective_id=0, has_side_effects=True, vmem_limit_bytes=KERNEL_MIB * 2 ** 20),
        cost_estimate=pl.CostEstimate(flops=2 * TOK * D * C, bytes_accessed=4 * 1024 * 1024, transcendentals=0),
    )(tokens, cotangent, norm_gain.reshape(1, D), replica_drift, exponents[0].T, own_rows, global_weight)
    return new_global, new_momentum.reshape(momentum.shape)


def solution(mesh):
    placed = (
        P(("rep", "fsdp"), None),
        P(("rep", "fsdp"), None),
        P(),
        P("rep", "fsdp", None),
        P("rep", "fsdp", None),
        P("fsdp", None),
        P("fsdp", "rep", None, None),
    )
    return jax.shard_map(
        body,
        mesh=mesh,
        in_specs=placed,
        out_specs=(P("fsdp", None), P("fsdp", "rep", None, None)),
        check_vma=False,
    )
```
